128 devices in a mesh: member: 4 (over z), space: 32 (over x, y, core).
Axes of the slice: x: 4, y: 4, z: 4, core: 2. Of those that a mesh axis runs over, the one named last changes fastest.
Arguments:
- background: bfloat16 [80, 20, 65536], P('member', None, 'space'), may hold values from -6 to 6
- perturbation: bfloat16 [80, 524288], P(None, ('member', 'space')), may hold values from -0.875 to 0.875
- innovation: float32 [524288], P(('member', 'space')), may hold values from -6 to 6
- obs_weight: float32 [524288], P(('member', 'space')), may hold values from 0.5 to 4
- route_dest: int32 [524288, 2], P(('member', 'space')), may hold values from 0 to 127, all different within a row; in each aligned block of 4096 rows (0 to 4095, 4096 to 8191, ...) at most 128 rows name the same one
- localization: float32 [2, 1, 524288], P(None, None, ('member', 'space')), may hold values from 0.05 to 1
Outputs:
- analysis: bfloat16 [80, 20, 65536], P('member', None, 'space')
The draws below stay inside these ranges and needn't reach their ends.
Inputs may be any that keep to these rules, and one draw needn't show every extreme that they name: `route_dest`: each observation names 2 different units. Within the rows of one device no unit is named by more than 128 rows, a bound that some block reaches.
All inputs are finite; a program needn't handle non-finite values.
Results may differ from the reference program's by a relative error of at most 0.0052.
Values may be sent and summed in bfloat16 or wider, within the bound.
A program may use at most 128 MiB of HBM per device.

```python
import math
import jax
import jax.numpy as jnp
import numpy as np
from jax import lax

K = 80
PATCH = 512
P_DEV = 1
OBS_DEV = 4096
TOP = 2
NS_ITERS = 16
CAP = 128
FL = 20
CELLS = 65536
OBS = 524288
SLOTS = 16384
N_MEMBER = 4
N_SPACE = 32
DEVICES = 128


def shard_levels(rng, shape, pieces, low, top_value):
    factor_of, own = 1.0, jax.random.fold_in(rng, 6)
    for dim, shards_of in pieces:
        heights = jnp.exp(jax.random.uniform(jax.random.fold_in(own, dim), (shards_of,), jnp.float32, low / len(pieces), top_value / len(pieces)))
        factor_of = factor_of * jnp.repeat(heights, shape[dim] // shards_of).reshape([-1 if axis == dim else 1 for axis in range(len(shape))])
    return factor_of


def assign_block(key, own, number, rows, count, top, reach, lean):
    order = jax.random.permutation(key, count)
    packed, ordinary = load_shares(count, rows * top, reach, lean, True), load_shares(count, rows * top, reach, lean, False)
    places = jnp.arange(count)

    def named(sizes, offset_by):
        used = int((sizes > 0).sum())
        fixed = max(1, used // 4)
        shifted = fixed + (places - fixed + offset_by * (used - fixed)) % max(1, count - fixed)
        return jnp.zeros((count,), jnp.int32).at[order[jnp.where(places < fixed, places, shifted)]].set(jnp.asarray(sizes, jnp.int32))

    sizes = jnp.where(number % 4 == 0, named(packed, number // 4), named(ordinary, number - number // 4 - 1))
    mixed = jax.random.permutation(jax.random.fold_in(own, 3), count)
    giver, receiver = mixed[0:count // 2 * 2:2], mixed[1:count // 2 * 2:2]
    margin = jnp.minimum(sizes[giver] - 1, reach - sizes[receiver]) // 2
    margin = jnp.where((giver == order[0]) | (receiver == order[0]) | (sizes[receiver] == 0), 0, jnp.maximum(margin, 0))
    shifted = jax.random.randint(jax.random.fold_in(own, 4), (count // 2,), 0, 1 << 20) % (margin + 1)
    sizes = sizes.at[giver].add(-shifted).at[receiver].add(shifted)
    labels = jnp.searchsorted(jnp.cumsum(sizes), jnp.arange(rows * top), side="right").astype(jnp.int32)
    table = labels.reshape(top, rows).T
    table = table[jax.random.permutation(jax.random.fold_in(own, 1), rows)]
    offset_by = jax.random.randint(jax.random.fold_in(own, 2), (rows, 1), 0, top)
    return jnp.take_along_axis(table, (jnp.arange(top)[None, :] + offset_by) % top, axis=1)


def load_shares(count, total, most, skew, full):
    loads = [(1 << 20) // math.isqrt(standing ** skew) + 1 for standing in range(1, count + 1)]
    largest = most if full else min(most, max(-(-total // count), total * loads[0] // sum(loads)))
    least = 1 if total - largest >= count - 1 else 0
    holding, spare = [largest] + [least] * (count - 1), total - largest - least * (count - 1)
    while spare > 0:
        movable = [i for i in range(1, count) if holding[i] < largest] or [i for i in range(1, count) if holding[i] < most]
        pool, budget = sum([loads[i] for i in movable]), spare
        for i in movable:
            addition = min(most - holding[i], max(1, budget * loads[i] // pool), spare)
            holding[i] = holding[i] + addition
            spare = spare - addition
    return np.array(holding)


def scatter_about(own_key, extent, spread, limit, split=(), held_as=jnp.bfloat16):
    level = shard_levels(own_key, extent, split, -0.22, 0.18) if split else 1.0
    result = jax.random.normal(own_key, extent, jnp.float32) * spread * level
    return jnp.minimum(jnp.maximum(result, -limit), limit).astype(held_as)


def setup_inputs(seed: int = 0) -> dict:
    splits = jax.random.split(jax.random.key(seed), 7)
    background = scatter_about(splits[0], (K, FL, CELLS), 1.0, 6.0, ((0, 4), (2, 32)))
    perturbation = scatter_about(splits[1], (K, OBS), (1.4 * K ** 0.5 * (TOP * OBS_DEV) ** -0.5), 0.875, ((1, 128),))
    innovation = scatter_about(splits[2], (OBS,), 1.0, 6.0, ((0, 128),), jnp.float32)
    obs_weight = jnp.clip(jnp.exp(math.log(4.0) - 2.0794415 * jax.random.uniform(splits[3], (OBS,), jnp.float32) ** shard_levels(splits[3], (OBS,), ((0, 128),), -0.2, 0.2)), 0.5, 4.0)
    route_dest_keys = jax.random.split(jax.random.fold_in(splits[4], 1), OBS // OBS_DEV)
    route_dest_turns = jax.random.permutation(jax.random.fold_in(splits[4], 3), OBS // OBS_DEV)
    route_dest = jax.vmap(lambda own, number: assign_block(jax.random.fold_in(splits[4], 2), own, number, OBS_DEV, DEVICES, TOP, CAP, 2))(route_dest_keys, route_dest_turns).reshape((OBS, TOP))
    localization = jnp.clip(jnp.exp(math.log(1.0) - 2.9957323 * jax.random.uniform(splits[5], (TOP, P_DEV, OBS), jnp.float32) ** shard_levels(splits[5], (TOP, P_DEV, OBS), ((2, 128),), -0.2, 0.2)), 0.05, 1.0)
    return dict(background=background, perturbation=perturbation, innovation=innovation, obs_weight=obs_weight, route_dest=route_dest, localization=localization)


def entry_terms(perturbation, innovation, obs_weight, localization, slot_ids, entries, reach_count):
    occupied = slot_ids < entries
    obs_index = jnp.where(occupied, slot_ids // reach_count, 0).astype(jnp.int32)
    route_index = jnp.where(occupied, slot_ids % reach_count, 0).astype(jnp.int32)
    columns = jnp.where(occupied[None, :], perturbation[:, obs_index], 0).astype(jnp.bfloat16)
    chosen = localization[route_index, :, obs_index].T
    scaled = obs_weight[obs_index][None, :] * chosen
    coef = jnp.where(occupied[None, :], scaled, 0.0).astype(jnp.bfloat16)
    weighted = jnp.where(occupied[None, :], scaled * innovation[obs_index][None, :], 0.0).astype(jnp.bfloat16)
    return (columns, coef, weighted)

def transform(gram_sum, right_side, members, steps_count):
    identity = jnp.eye(members, dtype=jnp.float32)
    system = gram_sum + (members - 1.0) * identity
    scale = jnp.linalg.norm(system, axis=(-2, -1))[..., None, None]
    start_pair = (system / scale, jnp.broadcast_to(identity, system.shape).astype(jnp.float32))

    def newton_step(index, pair):
        approx, inverse = pair
        half = 0.5 * (3.0 * identity - jnp.matmul(inverse, approx, precision=lax.Precision.HIGHEST))
        approx = jnp.matmul(approx, half, precision=lax.Precision.HIGHEST)
        inverse = jnp.matmul(half, inverse, precision=lax.Precision.HIGHEST)
        return (approx, inverse)
    final_pair = lax.fori_loop(0, steps_count, newton_step, start_pair)
    inverse_root = final_pair[1] / jnp.sqrt(scale)
    halfway = jnp.matmul(inverse_root, right_side[..., :, None], precision=lax.Precision.HIGHEST)
    mean_weights = jnp.matmul(inverse_root, halfway, precision=lax.Precision.HIGHEST)[..., 0]
    weights = mean_weights[..., :, None] + math.sqrt(members - 1.0) * inverse_root
    column_sum = lax.optimization_barrier(jnp.sum(weights, axis=-2, keepdims=True))
    mixing = weights + (1.0 - column_sum) / members
    return mixing.astype(jnp.bfloat16)

def reference(background, perturbation, innovation, obs_weight, route_dest, localization):
    entries = OBS * TOP
    targets = route_dest.reshape(entries).astype(jnp.int32)
    ordering = jnp.argsort(targets, stable=True).astype(jnp.int32)
    sorted_targets = targets[ordering]
    counts = jax.ops.segment_sum(jnp.ones((entries,), jnp.int32), targets, num_segments=DEVICES).astype(jnp.int32)
    starts = (jnp.cumsum(counts) - counts).astype(jnp.int32)
    position = jnp.arange(entries, dtype=jnp.int32) - starts[sorted_targets]
    slot_index = (sorted_targets * SLOTS + position).astype(jnp.int32)
    slot_table = jnp.full((DEVICES * SLOTS,), entries, jnp.int32).at[slot_index].set(ordering)
    slot_table = slot_table.reshape(DEVICES, SLOTS)

    def unit_gram(slot_ids):
        columns, coef, weighted = entry_terms(perturbation, innovation, obs_weight, localization, slot_ids, entries, TOP)
        column_vals = columns.astype(jnp.float32)
        gram_sum = jnp.einsum('ks,ps,ls->pkl', column_vals, coef.astype(jnp.float32), column_vals, precision=lax.Precision.HIGHEST)
        right_side = jnp.einsum('ks,ps->pk', column_vals, weighted.astype(jnp.float32), precision=lax.Precision.HIGHEST)
        return (gram_sum, right_side)
    gram_all, rhs_all = lax.map(unit_gram, slot_table)
    mixing = transform(gram_all.reshape(DEVICES * P_DEV, K, K), rhs_all.reshape(DEVICES * P_DEV, K), K, NS_ITERS)
    mixing = jnp.swapaxes(mixing.reshape(N_MEMBER, N_SPACE, P_DEV, K, K), 0, 1)
    state_blocks = background.reshape(K, FL, N_SPACE, N_MEMBER, P_DEV, PATCH)
    state_blocks = jnp.moveaxis(state_blocks, 2, 0)

    def apply_block(pair):
        block_state, block_mix = pair
        mixed = jnp.einsum('jfmpi,mpjk->kfmpi', block_state.astype(jnp.float32), block_mix.astype(jnp.float32))
        return mixed.astype(jnp.bfloat16)
    analysed = lax.map(apply_block, (state_blocks, mixing))
    return jnp.moveaxis(analysed, 0, 2).reshape(K, FL, CELLS)
```

```python
import math

import jax
import jax.numpy as jnp
from jax import lax
from jax.experimental import pallas as pl
from jax.experimental.pallas import tpu as pltpu
from jax.sharding import PartitionSpec as P

BF = jnp.bfloat16
F32 = jnp.float32
MESH = pl.DeviceIdType.MESH
NN = (((1,), (0,)), ((), ()))
NT = (((1,), (1,)), ((), ()))

K = 80
OBS = 4096
UNITS = 128
Z = 4
XY = 16
FL = 20
FQ = 5
PATCH = 512
NS_STEPS = 8

GROUPS = (
    ((0, 0, 80), (32, 32, 48)),
    ((8, 8, 72), (24, 24, 56)),
    ((16, 16, 64), (40, 40, 40), (56, 56, 24)),
    ((48, 48, 32), (64, 64, 16), (72, 72, 8)),
)
NG = len(GROUPS)
WIDTH = tuple(sum(n for _, _, n in blocks) for blocks in GROUPS)
RHS_LANE = WIDTH[-1]


def iota(shape, dim):
    return lax.broadcasted_iota(jnp.int32, shape, dim)


def dot(a, b, dims=NN, precision=None):
    return lax.dot_general(a, b, dims, preferred_element_type=F32, precision=precision)


def dot_exact(a, b):
    return dot(a, b, precision=lax.Precision.HIGHEST)


def build_weights(dest, weight, innovation, localization, coef, weighted):
    step = 512
    row = iota((UNITS, 1), 0)
    unit = (row % Z) * 32 + ((row % 64) // Z) * 2 + row // 64
    for start in range(0, OBS, step):
        at = slice(start, start + step)
        first = weight[:, at] * localization[0, :, at]
        second = weight[:, at] * localization[1, :, at]
        to_first = dest[0:1, at] == unit
        to_second = dest[1:2, at] == unit

        def pick(a, b):
            a, b = a.astype(BF).astype(F32), b.astype(BF).astype(F32)
            return jnp.where(to_first, a, jnp.where(to_second, b, 0.0)).astype(BF)

        coef[:, at] = pick(first, second)
        weighted[:, at] = pick(first * innovation[:, at], second * innovation[:, at])


def build_products(y, feats, group):
    step = 512
    for start in range(0, OBS, step):
        at = slice(start, start + step)
        row = 0
        for i in range(8):
            for k, l, n in GROUPS[group]:
                feats[row : row + n, at] = y[k + i : k + i + 1, at] * y[l : l + n, at]
                row += n


def inverse_root(system):
    eye = (iota((K, K), 0) == iota((K, K), 1)).astype(F32)
    upper = jnp.max(jnp.sum(jnp.abs(system), axis=1, keepdims=True), axis=0, keepdims=True)
    low = jnp.sqrt((K - 1.0) / upper)
    approx, inverse = system * (1.0 / upper), None
    for step in range(NS_STEPS):
        square = 3.0 / (1.0 + low + low * low)
        stretch = jnp.sqrt(square)
        product = approx if inverse is None else dot_exact(inverse, approx)
        half = (1.5 * stretch) * eye - (0.5 * stretch * square) * product
        low = 0.5 * stretch * low * (3.0 - square * low * low)
        if step < NS_STEPS - 1:
            approx = dot_exact(approx, half)
        inverse = half if inverse is None else dot_exact(half, inverse)
    return inverse * lax.rsqrt(upper)


def unpack_system(total):
    lane = iota((8, 128), 1)
    tiles = [None] * (K // 8)
    for g, blocks in enumerate(GROUPS):
        slots = total[8 * g : 8 * g + 8]
        offset = 0
        for k, l, n in blocks:
            rolled = pltpu.roll(slots, (l - offset) % 128, 1) if l != offset else slots
            tiles[k // 8] = jnp.where((lane >= l) & (lane < l + n), rolled, 0.0)
            offset += n
    upper = jnp.concatenate(tiles + [jnp.zeros((128 - K, 128), F32)], axis=0)
    row, col = iota((128, 128), 0), iota((128, 128), 1)
    above = jnp.where((row // 8) == (col // 8), 0.0, upper)
    gram = (upper + above.T)[:K, :K]
    eye = (iota((K, K), 0) == iota((K, K), 1)).astype(F32)
    slots = total[8 * (NG - 1) :]
    part = jnp.zeros((8, 128), F32)
    for i in range(K // 16):
        rolled = pltpu.roll(slots, (16 * i - RHS_LANE) % 128, 1)
        part = jnp.where((iota((8, 128), 0) == i) & (lane // 16 == i), rolled, part)
    right_side = jnp.sum(part, axis=0, keepdims=True)[:, :K]
    return gram + (K - 1.0) * eye, right_side


def mixing_t(root, right_side):
    halfway = jnp.sum(root * right_side, axis=1, keepdims=True)
    mean = jnp.sum(root * halfway, axis=0, keepdims=True)
    spread = math.sqrt(K - 1.0) * root
    column = jnp.sum(mean, axis=1, keepdims=True) + jnp.sum(spread, axis=1, keepdims=True)
    return (mean + spread + (1.0 - column) / K).astype(BF)


def kernel(
    bg, y_in, dest_in, weight_in, innovation_in, local_in, out,
    bgv, y, dest, weight, innovation, local, coef, weighted, feats, gbuf, gpeer,
    stage, stage16, plane, zsend, zrecv, prep, land, back, back_land,
    in_sem, core_s, core_r, plane_s, plane_r, z_s, z_r, bg_s, bg_r, back_s, back_r,
):
    z = lax.axis_index("member")
    s = lax.axis_index("space")
    core = lax.rem(s, 2)
    xy = lax.div(s, 2)

    def z_peer(d):
        return (lax.rem(z + d, Z), s)

    def plane_peer(d):
        return (z, 2 * lax.rem(xy + d, XY) + core)

    core_peer = (z, 2 * xy + 1 - core)

    barrier = pltpu.get_barrier_semaphore()
    for d in range(1, Z):
        pl.semaphore_signal(barrier, inc=1, device_id=z_peer(d), device_id_type=MESH)
    pl.semaphore_signal(barrier, inc=1, device_id=core_peer, device_id_type=MESH)
    for d in range(1, XY):
        pl.semaphore_signal(barrier, inc=1, device_id=plane_peer(d), device_id_type=MESH)

    loads = [
        pltpu.make_async_copy(src, dst, in_sem.at[i])
        for i, (src, dst) in enumerate(
            ((dest_in, dest), (weight_in, weight), (local_in, local), (innovation_in, innovation), (y_in, y), (bg, bgv))
        )
    ]
    for load in loads:
        load.start()

    def bg_copy(fq, d):
        return pltpu.make_async_remote_copy(
            prep.at[fq, d - 1], land.at[fq, z], bg_s.at[fq, d - 1], bg_r.at[fq, z], device_id=z_peer(d), device_id_type=MESH
        )

    def bg_arrival(fq, d):
        source = lax.rem(z + d, Z)
        return pltpu.make_async_remote_copy(
            prep.at[fq, d - 1], land.at[fq, source], bg_s.at[fq, d - 1], bg_r.at[fq, source], device_id=z_peer(d), device_id_type=MESH
        )

    def send_bg(fq):
        for d in (2, 1, 3):
            bg_copy(fq, d).start()

    def core_copy(g):
        return pltpu.make_async_remote_copy(
            gbuf.at[g, 1 - core], gpeer.at[g], core_s.at[g], core_r.at[g], device_id=core_peer, device_id_type=MESH
        )

    def plane_copy(g, d):
        return pltpu.make_async_remote_copy(
            stage16.at[g, lax.rem(xy + d, XY)], plane.at[g, xy], plane_s.at[g, d], plane_r.at[g, xy],
            device_id=plane_peer(d), device_id_type=MESH,
        )

    def plane_arrival(g, d):
        source = lax.rem(xy + d, XY)
        return pltpu.make_async_remote_copy(
            stage16.at[g, source], plane.at[g, source], plane_s.at[g, d], plane_r.at[g, source],
            device_id=plane_peer(d), device_id_type=MESH,
        )

    def z_copy(d):
        return pltpu.make_async_remote_copy(
            zsend.at[lax.rem(z + d, Z)], zrecv.at[z], z_s.at[d], z_r.at[z], device_id=z_peer(d), device_id_type=MESH
        )

    def z_arrival(d):
        source = lax.rem(z + d, Z)
        return pltpu.make_async_remote_copy(
            zsend.at[source], zrecv.at[source], z_s.at[d], z_r.at[source], device_id=z_peer(d), device_id_type=MESH
        )

    def back_copy(fq, d):
        return pltpu.make_async_remote_copy(
            back.at[fq, lax.rem(z + d, Z)], back_land.at[fq, z], back_s.at[fq, d - 1], back_r.at[fq, z],
            device_id=z_peer(d), device_id_type=MESH,
        )

    def back_arrival(fq, d):
        source = lax.rem(z + d, Z)
        return pltpu.make_async_remote_copy(
            back.at[fq, source], back_land.at[fq, source], back_s.at[fq, d - 1], back_r.at[fq, source],
            device_id=z_peer(d), device_id_type=MESH,
        )

    def partial_gram(g):
        width = WIDTH[g]
        buf = feats.at[g % 2]
        build_products(y, buf, g)
        tail = None
        if g == NG - 1:
            tail = dot(y[...], weighted[...], NT)
        for part in range(2):
            rows = 4 * width
            result = dot(buf[part * rows : (part + 1) * rows, :], coef[...], NT)
            for j in range(4):
                i = 4 * part + j
                slot = result[j * width : (j + 1) * width]
                if width < 128:
                    pieces = [slot]
                    filled = width
                    if i < K // 16:
                        pieces.append(tail[16 * i : 16 * i + 16])
                        filled += 16
                    pieces.append(jnp.zeros((128 - filled, UNITS), F32))
                    slot = jnp.concatenate(pieces, axis=0)
                turned = slot.T
                gbuf[g, 0, i] = turned[:64]
                gbuf[g, 1, i] = turned[64:]

    def send_plane(g):
        core_copy(g).wait_recv()
        for i in range(8):
            stage[g, pl.ds(i, 64, stride=8), :] = gbuf[g, core, i] + gpeer[g, i]
        stage16[g] = stage[g].reshape(XY, 32, 128).astype(BF)

        def start(d, carry):
            plane_copy(g, d).start()
            return carry

        lax.fori_loop(1, XY, start, 0)

    def sum_plane(g):
        def wait(d, carry):
            plane_arrival(g, d).wait_recv()
            return carry

        lax.fori_loop(1, XY, wait, 0)
        total = stage[g, pl.ds(pl.multiple_of(xy * 32, 32), 32), :]
        for d in range(1, XY):
            total = total + plane[g, lax.rem(xy + d, XY)].astype(F32)
        for t in range(Z):
            zsend[t, 8 * g : 8 * g + 8] = total[8 * t : 8 * t + 8]

    for load in loads[:5]:
        load.wait()
    build_weights(dest, weight, innovation, local, coef, weighted)
    partial_gram(0)

    loads[5].wait()
    for fq in range(FQ):
        rows = slice(4 * fq, 4 * fq + 4)
        for j in range(FL):
            to = slice(4 * j, 4 * j + 4)
            land[fq, z, to] = bgv[j, rows, pl.ds(pl.multiple_of(z * PATCH, PATCH), PATCH)]
            for d in range(1, Z):
                cells = pl.ds(pl.multiple_of(lax.rem(z + d, Z) * PATCH, PATCH), PATCH)
                prep[fq, d - 1, to] = bgv[j, rows, cells]

    pl.semaphore_wait(barrier, Z - 1 + 1 + XY - 1)
    core_copy(0).start()
    for fq in range(3):
        send_bg(fq)
    partial_gram(1)
    core_copy(1).start()
    send_plane(0)
    partial_gram(2)
    core_copy(2).start()
    send_plane(1)
    partial_gram(3)
    core_copy(3).start()
    send_plane(2)
    send_plane(3)
    expand = ((iota((4 * K, K), 0) // 4) == iota((4 * K, K), 1)).astype(BF)
    expand_t = (iota((K, 4 * K), 0) == (iota((K, 4 * K), 1) // 4)).astype(BF)
    for g in range(NG):
        sum_plane(g)
    for d in (2, 1, 3):
        z_copy(d).start()
    for fq in range(3, FQ):
        send_bg(fq)
    total = zsend[z]
    for d in range(1, Z):
        z_arrival(d).wait_recv()
        total = total + zrecv[lax.rem(z + d, Z)]

    system, right_side = unpack_system(total)
    mixing = mixing_t(inverse_root(system), right_side)
    wide = dot(dot(expand, mixing).astype(BF), expand_t)
    same = (iota((4 * K, 4 * K), 0) % 4) == (iota((4 * K, 4 * K), 1) % 4)
    spread = jnp.where(same, wide, 0.0).astype(BF)

    for fq in range(FQ):
        for d in (2, 1, 3):
            bg_arrival(fq, d).wait_recv()
        block = dot(spread, land[fq].reshape(Z * K, PATCH))
        back[fq] = block.astype(BF).reshape(Z, K, PATCH)
        for d in (2, 1, 3):
            back_copy(fq, d).start()

    def place(fq, m, ref):
        cells = pl.ds(pl.multiple_of(m * PATCH, PATCH), PATCH)
        for j in range(FL):
            out[j, 4 * fq : 4 * fq + 4, cells] = ref[fq, m, 4 * j : 4 * j + 4]

    for fq in range(FQ):
        place(fq, z, back)
    for fq in range(FQ):
        for d in (2, 1, 3):
            back_arrival(fq, d).wait_recv()
            place(fq, lax.rem(z + d, Z), back_land)

    for g in range(NG):
        core_copy(g).wait_send()

        def sent(d, carry):
            plane_copy(g, d).wait_send()
            return carry

        lax.fori_loop(1, XY, sent, 0)
    for d in range(1, Z):
        z_copy(d).wait_send()
        for fq in range(FQ):
            bg_copy(fq, d).wait_send()
            back_copy(fq, d).wait_send()


def per_device(background, perturbation, innovation, obs_weight, route_dest, localization):
    sem = pltpu.SemaphoreType.DMA
    scratch = [
        pltpu.VMEM((FL, FL, Z * PATCH), BF),
        pltpu.VMEM((K, OBS), BF),
        pltpu.VMEM((2, OBS), jnp.int32),
        pltpu.VMEM((1, OBS), F32),
        pltpu.VMEM((1, OBS), F32),
        pltpu.VMEM((2, 1, OBS), F32),
        pltpu.VMEM((UNITS, OBS), BF),
        pltpu.VMEM((UNITS, OBS), BF),
        pltpu.VMEM((2, 8 * 128, OBS), BF),
        pltpu.VMEM((NG, 2, 8, 64, 128), F32),
        pltpu.VMEM((NG, 8, 64, 128), F32),
        pltpu.VMEM((NG, 64 * 8, 128), F32),
        pltpu.VMEM((NG, XY, 32, 128), BF),
        pltpu.VMEM((NG, XY, 32, 128), BF),
        pltpu.VMEM((Z, 8 * NG, 128), F32),
        pltpu.VMEM((Z, 8 * NG, 128), F32),
        pltpu.VMEM((FQ, Z - 1, K, PATCH), BF),
        pltpu.VMEM((FQ, Z, K, PATCH), BF),
        pltpu.VMEM((FQ, Z, K, PATCH), BF),
        pltpu.VMEM((FQ, Z, K, PATCH), BF),
        sem((6,)),
        sem((NG,)),
        sem((NG,)),
        sem((NG, XY)),
        sem((NG, XY)),
        sem((Z,)),
        sem((Z,)),
        sem((FQ, Z)),
        sem((FQ, Z)),
        sem((FQ, Z)),
        sem((FQ, Z)),
    ]
    return pl.pallas_call(
        kernel,
        name="analysis",
        out_shape=jax.ShapeDtypeStruct(background.shape, BF),
        in_specs=[pl.BlockSpec(memory_space=pl.ANY)] * 6,
        out_specs=pl.BlockSpec(memory_space=pltpu.VMEM),
        scratch_shapes=scratch,
        compiler_params=pltpu.CompilerParams(collective_id=0, has_side_effects=True, vmem_limit_bytes=52 << 20),
    )(
        background,
        perturbation,
        route_dest.T,
        obs_weight.reshape(1, OBS),
        innovation.reshape(1, OBS),
        localization,
    )


def solution(mesh):
    in_specs = (
        P("member", None, "space"),
        P(None, ("member", "space")),
        P(("member", "space")),
        P(("member", "space")),
        P(("member", "space"), None),
        P(None, None, ("member", "space")),
    )
    out_specs = P("member", None, "space")
    return jax.shard_map(per_device, mesh=mesh, in_specs=in_specs, out_specs=out_specs, check_vma=False)
```

```python
import math

import jax
import jax.numpy as jnp
from jax import lax
from jax.experimental import pallas as pl
from jax.experimental.pallas import tpu as pltpu
from jax.sharding import PartitionSpec as P

BF = jnp.bfloat16
F32 = jnp.float32
MESH = pl.DeviceIdType.MESH
NN = (((1,), (0,)), ((), ()))
NT = (((1,), (1,)), ((), ()))

K = 80
OBS = 4096
UNITS = 128
Z = 4
XY = 16
HALF = UNITS // 2
FL = 20
FQ = 5
PATCH = 512
NS_STEPS = 8
VMEM_LIMIT = 63 << 20

GROUPS = (
    ((0, 0, 80), (32, 32, 48)),
    ((8, 8, 72), (24, 24, 56)),
    ((16, 16, 64), (40, 40, 40), (56, 56, 24)),
    ((48, 48, 32), (64, 64, 16), (72, 72, 8)),
)
NG = len(GROUPS)
WIDTH = tuple(sum(n for _, _, n in blocks) for blocks in GROUPS)
RHS_LANE = WIDTH[-1]


def iota(shape, dim):
    return lax.broadcasted_iota(jnp.int32, shape, dim)


def dot(a, b, dims=NN, precision=None):
    return lax.dot_general(a, b, dims, preferred_element_type=F32, precision=precision)


def dot_exact(a, b):
    return dot(a, b, precision=lax.Precision.HIGHEST)


def build_weights(dest, weight, innovation, localization, coef, weighted):
    step = 512
    row = iota((UNITS, 1), 0)
    unit = (row % Z) * 32 + ((row % HALF) // Z) * 2 + row // HALF
    for start in range(0, OBS, step):
        at = slice(start, start + step)
        first = weight[:, at] * localization[0, :, at]
        second = weight[:, at] * localization[1, :, at]
        to_first = dest[0:1, at] == unit
        to_second = dest[1:2, at] == unit

        def pick(a, b):
            a, b = a.astype(BF).astype(F32), b.astype(BF).astype(F32)
            return jnp.where(to_first, a, jnp.where(to_second, b, 0.0)).astype(BF)

        coef[:, at] = pick(first, second)
        weighted[:, at] = pick(first * innovation[:, at], second * innovation[:, at])


def build_products(y, feats, group):
    step = 512
    for start in range(0, OBS, step):
        at = slice(start, start + step)
        row = 0
        for i in range(8):
            for k, l, n in GROUPS[group]:
                feats[row : row + n, at] = y[k + i : k + i + 1, at] * y[l : l + n, at]
                row += n


def inverse_root(system):
    eye = (iota((K, K), 0) == iota((K, K), 1)).astype(F32)
    upper = jnp.max(jnp.sum(jnp.abs(system), axis=1, keepdims=True), axis=0, keepdims=True)
    low = jnp.sqrt((K - 1.0) / upper)
    approx, inverse = system * (1.0 / upper), None
    for step in range(NS_STEPS):
        square = 3.0 / (1.0 + low + low * low)
        stretch = jnp.sqrt(square)
        product = approx if inverse is None else dot_exact(inverse, approx)
        half = (1.5 * stretch) * eye - (0.5 * stretch * square) * product
        low = 0.5 * stretch * low * (3.0 - square * low * low)
        if step < NS_STEPS - 1:
            approx = dot_exact(approx, half)
        inverse = half if inverse is None else dot_exact(half, inverse)
    return inverse * lax.rsqrt(upper)


def unpack_system(total):
    lane = iota((8, 128), 1)
    tiles = [None] * (K // 8)
    for g, blocks in enumerate(GROUPS):
        slots = total[8 * g : 8 * g + 8]
        offset = 0
        for k, l, n in blocks:
            rolled = pltpu.roll(slots, (l - offset) % 128, 1) if l != offset else slots
            tiles[k // 8] = jnp.where((lane >= l) & (lane < l + n), rolled, 0.0)
            offset += n
    upper = jnp.concatenate(tiles + [jnp.zeros((128 - K, 128), F32)], axis=0)
    row, col = iota((128, 128), 0), iota((128, 128), 1)
    above = jnp.where((row // 8) == (col // 8), 0.0, upper)
    gram = (upper + above.T)[:K, :K]
    eye = (iota((K, K), 0) == iota((K, K), 1)).astype(F32)
    slots = total[8 * (NG - 1) :]
    part = jnp.zeros((8, 128), F32)
    for i in range(K // 16):
        rolled = pltpu.roll(slots, (16 * i - RHS_LANE) % 128, 1) + pltpu.roll(slots, (16 * i - RHS_LANE - 16) % 128, 1)
        part = jnp.where((iota((8, 128), 0) == i) & (lane // 16 == i), rolled, part)
    right_side = jnp.sum(part, axis=0, keepdims=True)[:, :K]
    return gram + (K - 1.0) * eye, right_side


def mixing_t(root, right_side):
    halfway = jnp.sum(root * right_side, axis=1, keepdims=True)
    mean = jnp.sum(root * halfway, axis=0, keepdims=True)
    spread = math.sqrt(K - 1.0) * root
    column = jnp.sum(mean, axis=1, keepdims=True) + jnp.sum(spread, axis=1, keepdims=True)
    return (mean + spread + (1.0 - column) / K).astype(BF)


def kernel(
    bg, y_in, dest_in, weight_in, innovation_in, local_in, out,
    bgv, y, dest, weight, innovation, local, coef, weighted, feats,
    stage, peer_stage, stage16, plane, zsend, zrecv, prep, land, back,
    in_sem, core_s, core_r, plane_s, plane_r, z_s, z_r, bg_s, bg_r, back_s, back_r, own_s,
):
    z = lax.axis_index("member")
    s = lax.axis_index("space")
    core = lax.rem(s, 2)
    xy = lax.div(s, 2)

    def z_peer(d):
        return (lax.rem(z + d, Z), s)

    def plane_chip(d):
        return lax.rem(lax.div(xy, 4) + d // 4, 4) * 4 + lax.rem(lax.rem(xy, 4) + d % 4, 4)

    def plane_peer(d):
        return (z, 2 * plane_chip(d) + core)

    core_peer = (z, 2 * xy + 1 - core)

    barrier = pltpu.get_barrier_semaphore()
    far_first = sorted(range(1, XY), key=lambda d: -(min(d // 4, 4 - d // 4) + min(d % 4, 4 - d % 4)))
    peers = [plane_peer(d) for d in far_first] + [z_peer(d) for d in (2, 1, 3)] + [core_peer]
    for peer in peers:
        pl.semaphore_signal(barrier, inc=1, device_id=peer, device_id_type=MESH)

    loads = [
        pltpu.make_async_copy(src, dst, in_sem.at[i])
        for i, (src, dst) in enumerate(
            ((dest_in, dest), (weight_in, weight), (local_in, local), (innovation_in, innovation), (y_in, y), (bg, bgv))
        )
    ]
    for load in loads:
        load.start()

    def remote(src, dst, send, recv, peer):
        return pltpu.make_async_remote_copy(src, dst, send, recv, device_id=peer, device_id_type=MESH)

    branch = pl.when(z >= 0)

    def send_bg(*fqs):
        @branch
        def _():
            for fq in fqs:
                send_bg_group(fq)

    def send_bg_group(fq):
        for d in (2, 1, 3):
            remote(prep.at[fq, d - 1], land.at[fq, z], bg_s, bg_r.at[fq], z_peer(d)).start()

    def bg_arrivals(fq):
        return remote(prep.at[fq], land.at[fq, 0 : Z - 1], bg_s, bg_r.at[fq], z_peer(1))

    def bg_sends():
        return remote(prep, prep, bg_s, bg_r.at[0], z_peer(1))

    def core_copy(g):
        return remote(stage.at[g, 1 - core], peer_stage.at[g], core_s.at[g], core_r.at[g], core_peer)

    def send_core(g):
        @branch
        def _():
            core_copy(g).start()

    def send_plane(g):
        core_copy(g).wait_recv()
        total = stage[g, core] + peer_stage[g]
        if g == NG - 1:
            rest = pltpu.roll(total - total.astype(BF).astype(F32), 16, 1)
            lane = iota(total.shape, 1)
            total = jnp.where((lane >= RHS_LANE + 16) & (lane < RHS_LANE + 32), rest, total)
        stage16[g] = total.reshape(XY, 8 * Z, 128).astype(BF)

        @branch
        def _():
            for d in far_first:
                remote(stage16.at[g, plane_chip(d)], plane.at[g, d - 1], plane_s.at[g], plane_r.at[g], plane_peer(d)).start()

    def plane_all(g):
        return remote(plane.at[g], plane.at[g], plane_s.at[g], plane_r.at[g], plane_peer(1))

    def send_column():
        @branch
        def _():
            for d in (2, 1, 3):
                remote(zsend.at[lax.rem(z + d, Z)], zrecv.at[d - 1], z_s, z_r, z_peer(d)).start()

    def column_all():
        return remote(zrecv, zrecv, z_s, z_r, z_peer(1))

    def send_back(fq):
        @branch
        def _():
            for d in (2, 1, 3):
                remote(back.at[fq, lax.rem(z + d, Z)], out.at[fq, z], back_s, back_r, z_peer(d)).start()
            own_copy(fq).start()

    def back_all():
        return remote(back.at[:, 0 : Z - 1], out.at[:, 0 : Z - 1], back_s, back_r, z_peer(1))

    def own_all():
        return pltpu.make_async_copy(back.at[:, 0], out.at[:, 0], own_s)

    def own_copy(fq):
        return pltpu.make_async_copy(back.at[fq, z], out.at[fq, z], own_s)

    def partial_gram(g):
        width = WIDTH[g]
        buf = feats.at[g % 2]
        build_products(y, buf, g)
        tail = None
        if g == NG - 1:
            tail = dot(y[...], weighted[...], NT)
        for part in range(2):
            rows = 4 * width
            result = dot(buf[part * rows : (part + 1) * rows, :], coef[...], NT)
            for j in range(4):
                i = 4 * part + j
                slot = result[j * width : (j + 1) * width]
                if width < 128:
                    pieces = [slot]
                    filled = width
                    if i < K // 16:
                        pieces.append(tail[16 * i : 16 * i + 16])
                        filled += 16
                    pieces.append(jnp.zeros((128 - filled, UNITS), F32))
                    slot = jnp.concatenate(pieces, axis=0)
                turned = slot.T
                stage[g, 0, pl.ds(i, HALF, stride=8), :] = turned[:HALF]
                stage[g, 1, pl.ds(i, HALF, stride=8), :] = turned[HALF:]

    def sum_plane(g):
        plane_all(g).wait_recv()
        total = stage16[g, xy].astype(F32)
        for d in range(XY - 1):
            total = total + plane[g, d].astype(F32)
        for t in range(Z):
            zsend[t, 8 * g : 8 * g + 8] = total[8 * t : 8 * t + 8]

    for load in loads[:4]:
        load.wait()
    build_weights(dest, weight, innovation, local, coef, weighted)
    loads[4].wait()
    partial_gram(0)
    loads[5].wait()
    for fq in range(FQ):
        rows = slice(4 * fq, 4 * fq + 4)
        for j in range(FL):
            to = slice(4 * j, 4 * j + 4)
            land[fq, z, to] = bgv[j, rows, pl.ds(pl.multiple_of(z * PATCH, PATCH), PATCH)]
            for d in range(1, Z):
                cells = pl.ds(pl.multiple_of(lax.rem(z + d, Z) * PATCH, PATCH), PATCH)
                prep[fq, d - 1, to] = bgv[j, rows, cells]

    pl.semaphore_wait(barrier, len(peers))
    send_core(0)
    send_bg(0, 1, 2)
    for g in range(1, NG):
        partial_gram(g)
        send_core(g)
        send_plane(g - 1)
    send_plane(NG - 1)
    expand_t = (iota((K, 4 * K), 0) == (iota((K, 4 * K), 1) // 4)).astype(BF)
    for g in range(NG):
        sum_plane(g)
    send_column()
    send_bg(3, 4)
    total = zsend[z]
    column_all().wait_recv()
    for d in range(Z - 1):
        total = total + zrecv[d]

    system, right_side = unpack_system(total)
    mixing = mixing_t(inverse_root(system), right_side)
    wide = jnp.broadcast_to(dot(mixing, expand_t)[:, None, :], (K, 4, 4 * K)).reshape(4 * K, 4 * K)
    same = (iota((4 * K, 4 * K), 0) % 4) == (iota((4 * K, 4 * K), 1) % 4)
    spread = jnp.where(same, wide, 0.0).astype(BF)

    for fq in range(FQ):
        bg_arrivals(fq).wait_recv()
        block = dot(spread, land[fq].reshape(Z * K, PATCH))
        back[fq] = block.astype(BF).reshape(Z, K, PATCH)
        send_back(fq)

    for g in range(NG):
        core_copy(g).wait_send()
        plane_all(g).wait_send()
    column_all().wait_send()
    bg_sends().wait_send()
    own_all().wait()
    back_all().wait()


def unpack(dense, out, piece, whole, load_sem, store_sem):
    loads = [pltpu.make_async_copy(dense.at[:, m], piece.at[:, m], load_sem.at[m]) for m in range(Z)]
    for load in loads:
        load.start()
    stores = []
    for m in range(Z):
        loads[m].wait()
        cells = slice(m * PATCH, (m + 1) * PATCH)
        for fq in range(FQ):
            for j in range(FL):
                whole[j, 4 * fq : 4 * fq + 4, cells] = piece[fq, m, 4 * j : 4 * j + 4]
        stores.append(pltpu.make_async_copy(whole.at[:, :, cells], out.at[:, :, cells], store_sem.at[m]))
        stores[-1].start()
    for store in stores:
        store.wait()


def per_device(background, perturbation, innovation, obs_weight, route_dest, localization):
    sem = pltpu.SemaphoreType.DMA
    scratch = [
        pltpu.VMEM((FL, FL, Z * PATCH), BF),
        pltpu.VMEM((K, OBS), BF),
        pltpu.VMEM((2, OBS), jnp.int32),
        pltpu.VMEM((1, OBS), F32),
        pltpu.VMEM((1, OBS), F32),
        pltpu.VMEM((2, 1, OBS), F32),
        pltpu.VMEM((UNITS, OBS), BF),
        pltpu.VMEM((UNITS, OBS), BF),
        pltpu.VMEM((2, 8 * 128, OBS), BF),
        pltpu.VMEM((NG, 2, HALF * 8, 128), F32),
        pltpu.VMEM((NG, HALF * 8, 128), F32),
        pltpu.VMEM((NG, XY, 8 * Z, 128), BF),
        pltpu.VMEM((NG, XY - 1, 8 * Z, 128), BF),
        pltpu.VMEM((Z, 8 * NG, 128), F32),
        pltpu.VMEM((Z - 1, 8 * NG, 128), F32),
        pltpu.VMEM((FQ, Z - 1, K, PATCH), BF),
        pltpu.VMEM((FQ, Z, K, PATCH), BF),
        pltpu.VMEM((FQ, Z, K, PATCH), BF),
        sem((6,)),
        sem((NG,)),
        sem((NG,)),
        sem((NG,)),
        sem((NG,)),
        sem,
        sem,
        sem,
        sem((FQ,)),
        sem,
        sem,
        sem,
    ]
    analysed = pl.pallas_call(
        kernel,
        name="analysis",
        out_shape=jax.ShapeDtypeStruct((FQ, Z, K, PATCH), BF),
        in_specs=[pl.BlockSpec(memory_space=pl.ANY)] * 6,
        out_specs=pl.BlockSpec(memory_space=pl.ANY),
        scratch_shapes=scratch,
        compiler_params=pltpu.CompilerParams(collective_id=0, has_side_effects=True, vmem_limit_bytes=VMEM_LIMIT),
    )(
        background,
        perturbation,
        route_dest.T,
        obs_weight.reshape(1, OBS),
        innovation.reshape(1, OBS),
        localization,
    )
    return pl.pallas_call(
        unpack,
        name="unpack",
        out_shape=jax.ShapeDtypeStruct(background.shape, BF),
        in_specs=[pl.BlockSpec(memory_space=pl.ANY)],
        out_specs=pl.BlockSpec(memory_space=pl.ANY),
        scratch_shapes=[
            pltpu.VMEM((FQ, Z, K, PATCH), BF),
            pltpu.VMEM((FL, FL, Z * PATCH), BF),
            sem((Z,)),
            sem((Z,)),
        ],
        compiler_params=pltpu.CompilerParams(vmem_limit_bytes=VMEM_LIMIT),
    )(analysed)


def solution(mesh):
    in_specs = (
        P("member", None, "space"),
        P(None, ("member", "space")),
        P(("member", "space")),
        P(("member", "space")),
        P(("member", "space"), None),
        P(None, None, ("member", "space")),
    )
    out_specs = P("member", None, "space")
    return jax.shard_map(per_device, mesh=mesh, in_specs=in_specs, out_specs=out_specs, check_vma=False)
```

```python
import math

import jax
import jax.numpy as jnp
from jax import lax
from jax.experimental import pallas as pl
from jax.experimental.pallas import tpu as pltpu
from jax.sharding import PartitionSpec as P

BF = jnp.bfloat16
F32 = jnp.float32
MESH = pl.DeviceIdType.MESH
NN = (((1,), (0,)), ((), ()))
NT = (((1,), (1,)), ((), ()))

K = 80
OBS = 4096
UNITS = 128
Z = 4
XY = 16
HALF = UNITS // 2
FL = 20
FQ = 5
PATCH = 512
NS_STEPS = 8
BG_PARTS = ((0, 4), (4, FQ))
BACK_PARTS = ((0, 1), (1, 3), (3, FQ))
VMEM_LIMIT = 63 << 20

GROUPS = (
    ((0, 0, 80), (32, 32, 48)),
    ((8, 8, 72), (24, 24, 56)),
    ((16, 16, 64), (40, 40, 40), (56, 56, 24)),
    ((48, 48, 32), (64, 64, 16), (72, 72, 8)),
)
NG = len(GROUPS)
WIDTH = tuple(sum(n for _, _, n in blocks) for blocks in GROUPS)
RHS_LANE = WIDTH[-1]


def iota(shape, dim):
    return lax.broadcasted_iota(jnp.int32, shape, dim)


def dot(a, b, dims=NN, precision=None):
    return lax.dot_general(a, b, dims, preferred_element_type=F32, precision=precision)


def dot_exact(a, b):
    return dot(a, b, precision=lax.Precision.HIGHEST)


def build_weights(dest, weight, innovation, localization, coef, weighted):
    step = 512
    row = iota((UNITS, 1), 0)
    unit = (row % Z) * 32 + ((row % HALF) // Z) * 2 + row // HALF
    for start in range(0, OBS, step):
        at = slice(start, start + step)
        first = weight[:, at] * localization[0, :, at]
        second = weight[:, at] * localization[1, :, at]
        to_first = dest[0:1, at] == unit
        to_second = dest[1:2, at] == unit

        def pick(a, b):
            a, b = a.astype(BF).astype(F32), b.astype(BF).astype(F32)
            return jnp.where(to_first, a, jnp.where(to_second, b, 0.0)).astype(BF)

        coef[:, at] = pick(first, second)
        weighted[:, at] = pick(first * innovation[:, at], second * innovation[:, at])


def build_products(y, feats, group):
    step = 512
    for start in range(0, OBS, step):
        at = slice(start, start + step)
        row = 0
        for i in range(8):
            for k, l, n in GROUPS[group]:
                feats[row : row + n, at] = y[k + i : k + i + 1, at] * y[l : l + n, at]
                row += n


def inverse_root(system):
    eye = (iota((K, K), 0) == iota((K, K), 1)).astype(F32)
    upper = jnp.max(jnp.sum(jnp.abs(system), axis=1, keepdims=True), axis=0, keepdims=True)
    low = jnp.sqrt((K - 1.0) / upper)
    approx, inverse = system * (1.0 / upper), None
    for step in range(NS_STEPS):
        square = 3.0 / (1.0 + low + low * low)
        stretch = jnp.sqrt(square)
        product = approx if inverse is None else dot_exact(inverse, approx)
        half = (1.5 * stretch) * eye - (0.5 * stretch * square) * product
        low = 0.5 * stretch * low * (3.0 - square * low * low)
        if step < NS_STEPS - 1:
            approx = dot_exact(approx, half)
        inverse = half if inverse is None else dot_exact(half, inverse)
    return inverse * lax.rsqrt(upper)


def unpack_system(total):
    lane = iota((8, 128), 1)
    tiles = [None] * (K // 8)
    for g, blocks in enumerate(GROUPS):
        slots = total[8 * g : 8 * g + 8]
        offset = 0
        for k, l, n in blocks:
            rolled = pltpu.roll(slots, (l - offset) % 128, 1) if l != offset else slots
            tiles[k // 8] = jnp.where((lane >= l) & (lane < l + n), rolled, 0.0)
            offset += n
    upper = jnp.concatenate(tiles + [jnp.zeros((128 - K, 128), F32)], axis=0)
    row, col = iota((128, 128), 0), iota((128, 128), 1)
    above = jnp.where((row // 8) == (col // 8), 0.0, upper)
    gram = (upper + above.T)[:K, :K]
    eye = (iota((K, K), 0) == iota((K, K), 1)).astype(F32)
    slots = total[8 * (NG - 1) :]
    part = jnp.zeros((8, 128), F32)
    for i in range(K // 16):
        rolled = pltpu.roll(slots, (16 * i - RHS_LANE) % 128, 1) + pltpu.roll(slots, (16 * i - RHS_LANE - 16) % 128, 1)
        part = jnp.where((iota((8, 128), 0) == i) & (lane // 16 == i), rolled, part)
    right_side = jnp.sum(part, axis=0, keepdims=True)[:, :K]
    return gram + (K - 1.0) * eye, right_side


def mixing_t(root, right_side):
    halfway = jnp.sum(root * right_side, axis=1, keepdims=True)
    mean = jnp.sum(root * halfway, axis=0, keepdims=True)
    spread = math.sqrt(K - 1.0) * root
    column = jnp.sum(mean, axis=1, keepdims=True) + jnp.sum(spread, axis=1, keepdims=True)
    return (mean + spread + (1.0 - column) / K).astype(BF)


def kernel(
    bg, y_in, dest_in, weight_in, innovation_in, local_in, out,
    bgv, y, dest, weight, innovation, local, coef, weighted, feats,
    stage, peer_stage, stage16, plane, zsend, zrecv, prep, land, back,
    in_sem, core_s, core_r, plane_s, plane_r, z_s, z_r, bg_s, bg_r, back_s, back_r, own_s,
):
    z = lax.axis_index("member")
    s = lax.axis_index("space")
    core = lax.rem(s, 2)
    xy = lax.div(s, 2)

    def z_peer(d):
        return (lax.rem(z + d, Z), s)

    def plane_chip(d):
        return lax.rem(lax.div(xy, 4) + d // 4, 4) * 4 + lax.rem(lax.rem(xy, 4) + d % 4, 4)

    def plane_peer(d):
        return (z, 2 * plane_chip(d) + core)

    core_peer = (z, 2 * xy + 1 - core)

    loads = [
        pltpu.make_async_copy(src, dst, in_sem.at[i])
        for i, (src, dst) in enumerate(
            ((dest_in, dest), (weight_in, weight), (local_in, local), (innovation_in, innovation), (y_in, y), (bg, bgv))
        )
    ]
    for load in loads:
        load.start()

    barrier = pltpu.get_barrier_semaphore()
    far_first = sorted(range(1, XY), key=lambda d: -(min(d // 4, 4 - d // 4) + min(d % 4, 4 - d % 4)))
    peers = [plane_peer(d) for d in far_first] + [z_peer(d) for d in (2, 1, 3)] + [core_peer]
    for peer in peers:
        pl.semaphore_signal(barrier, inc=1, device_id=peer, device_id_type=MESH)


    def remote(src, dst, send, recv, peer):
        return pltpu.make_async_remote_copy(src, dst, send, recv, device_id=peer, device_id_type=MESH)

    branch = pl.when(z >= 0)

    def send_bg(part):
        fqs = slice(*BG_PARTS[part])

        @branch
        def _():
            for d in (2, 1, 3):
                remote(prep.at[fqs, d - 1], land.at[fqs, z], bg_s, bg_r.at[part], z_peer(d)).start()

    def bg_arrivals(part):
        fqs = slice(*BG_PARTS[part])
        return remote(prep.at[fqs], land.at[fqs, 0 : Z - 1], bg_s, bg_r.at[part], z_peer(1))

    def bg_sends():
        return remote(prep, prep, bg_s, bg_r.at[0], z_peer(1))

    def core_copy(g):
        return remote(stage.at[g, 1 - core], peer_stage.at[g], core_s.at[g], core_r.at[g], core_peer)

    def send_core(g):
        @branch
        def _():
            core_copy(g).start()

    def send_plane(g):
        core_copy(g).wait_recv()
        total = stage[g, core] + peer_stage[g]
        if g == NG - 1:
            rest = pltpu.roll(total - total.astype(BF).astype(F32), 16, 1)
            lane = iota(total.shape, 1)
            total = jnp.where((lane >= RHS_LANE + 16) & (lane < RHS_LANE + 32), rest, total)
        stage16[g] = total.reshape(XY, 8 * Z, 128).astype(BF)

        @branch
        def _():
            for d in far_first:
                remote(stage16.at[g, plane_chip(d)], plane.at[g, d - 1], plane_s.at[g], plane_r.at[g], plane_peer(d)).start()

    def plane_all(g):
        return remote(plane.at[g], plane.at[g], plane_s.at[g], plane_r.at[g], plane_peer(1))

    def send_column():
        @branch
        def _():
            for d in (2, 1, 3):
                remote(zsend.at[lax.rem(z + d, Z)], zrecv.at[d - 1], z_s, z_r, z_peer(d)).start()

    def column_all():
        return remote(zrecv, zrecv, z_s, z_r, z_peer(1))

    def own_copy(fqs):
        return pltpu.make_async_copy(back.at[fqs, z], out.at[fqs, z], own_s)

    def send_back(part):
        fqs = slice(*BACK_PARTS[part])

        @branch
        def _():
            for d in (2, 1, 3):
                remote(back.at[fqs, lax.rem(z + d, Z)], out.at[fqs, z], back_s, back_r, z_peer(d)).start()
            own_copy(fqs).start()

    def back_all():
        return remote(back.at[:, 0 : Z - 1], out.at[:, 0 : Z - 1], back_s, back_r, z_peer(1))

    def own_all():
        return pltpu.make_async_copy(back.at[:, 0], out.at[:, 0], own_s)

    def partial_gram(g, parts=(0, 1)):
        width = WIDTH[g]
        buf = feats.at[g % 2]
        if 0 in parts:
            build_products(y, buf, g)
        tail = None
        if g == NG - 1:
            tail = dot(y[...], weighted[...], NT)
        for part in parts:
            rows = 4 * width
            result = dot(buf[part * rows : (part + 1) * rows, :], coef[...], NT)
            for j in range(4):
                i = 4 * part + j
                slot = result[j * width : (j + 1) * width]
                if width < 128:
                    pieces = [slot]
                    filled = width
                    if i < K // 16:
                        pieces.append(tail[16 * i : 16 * i + 16])
                        filled += 16
                    pieces.append(jnp.zeros((128 - filled, UNITS), F32))
                    slot = jnp.concatenate(pieces, axis=0)
                turned = slot.T
                stage[g, 0, pl.ds(i, HALF, stride=8), :] = turned[:HALF]
                stage[g, 1, pl.ds(i, HALF, stride=8), :] = turned[HALF:]

    def sum_plane(g):
        plane_all(g).wait_recv()
        total = stage16[g, xy].astype(F32)
        for d in range(XY - 1):
            total = total + plane[g, d].astype(F32)
        for t in range(Z):
            zsend[t, 8 * g : 8 * g + 8] = total[8 * t : 8 * t + 8]

    for load in loads[:4]:
        load.wait()
    build_weights(dest, weight, innovation, local, coef, weighted)
    loads[4].wait()
    partial_gram(0)
    loads[5].wait()
    for fq in range(FQ):
        rows = slice(4 * fq, 4 * fq + 4)
        for j in range(FL):
            to = slice(4 * j, 4 * j + 4)
            land[fq, z, to] = bgv[j, rows, pl.ds(pl.multiple_of(z * PATCH, PATCH), PATCH)]
            for d in range(1, Z):
                cells = pl.ds(pl.multiple_of(lax.rem(z + d, Z) * PATCH, PATCH), PATCH)
                prep[fq, d - 1, to] = bgv[j, rows, cells]

    pl.semaphore_wait(barrier, len(peers))
    send_core(0)
    send_bg(0)
    for g in range(1, NG):
        partial_gram(g)
        send_core(g)
        send_plane(g - 1)
    send_plane(NG - 1)
    expand_t = (iota((K, 4 * K), 0) == (iota((K, 4 * K), 1) // 4)).astype(BF)
    for g in range(NG):
        sum_plane(g)
    send_column()
    send_bg(1)
    total = zsend[z]
    column_all().wait_recv()
    for d in range(Z - 1):
        total = total + zrecv[d]

    system, right_side = unpack_system(total)
    mixing = mixing_t(inverse_root(system), right_side)
    wide = jnp.broadcast_to(dot(mixing, expand_t)[:, None, :], (K, 4, 4 * K)).reshape(4 * K, 4 * K)
    same = (iota((4 * K, 4 * K), 0) % 4) == (iota((4 * K, 4 * K), 1) % 4)
    spread = jnp.where(same, wide, 0.0).astype(BF)

    bg_arrivals(0).wait_recv()
    for part, (first, last) in enumerate(BACK_PARTS):
        if last == FQ:
            bg_arrivals(1).wait_recv()
        for fq in range(first, last):
            block = dot(spread, land[fq].reshape(Z * K, PATCH))
            back[fq] = block.astype(BF).reshape(Z, K, PATCH)
        send_back(part)

    for g in range(NG):
        core_copy(g).wait_send()
        plane_all(g).wait_send()
    column_all().wait_send()
    bg_sends().wait_send()
    own_all().wait()
    back_all().wait()


def unpack(dense, out, piece, whole, load_sem, store_sem):
    loads = [pltpu.make_async_copy(dense.at[:, m], piece.at[:, m], load_sem.at[m]) for m in range(Z)]
    for load in loads:
        load.start()
    stores = []
    for m in range(Z):
        loads[m].wait()
        cells = slice(m * PATCH, (m + 1) * PATCH)
        for fq in range(FQ):
            for j in range(FL):
                whole[j, 4 * fq : 4 * fq + 4, cells] = piece[fq, m, 4 * j : 4 * j + 4]
        stores.append(pltpu.make_async_copy(whole.at[:, :, cells], out.at[:, :, cells], store_sem.at[m]))
        stores[-1].start()
    for store in stores:
        store.wait()


def per_device(background, perturbation, innovation, obs_weight, route_dest, localization):
    sem = pltpu.SemaphoreType.DMA
    scratch = [
        pltpu.VMEM((FL, FL, Z * PATCH), BF),
        pltpu.VMEM((K, OBS), BF),
        pltpu.VMEM((2, OBS), jnp.int32),
        pltpu.VMEM((1, OBS), F32),
        pltpu.VMEM((1, OBS), F32),
        pltpu.VMEM((2, 1, OBS), F32),
        pltpu.VMEM((UNITS, OBS), BF),
        pltpu.VMEM((UNITS, OBS), BF),
        pltpu.VMEM((2, 8 * 128, OBS), BF),
        pltpu.VMEM((NG, 2, HALF * 8, 128), F32),
        pltpu.VMEM((NG, HALF * 8, 128), F32),
        pltpu.VMEM((NG, XY, 8 * Z, 128), BF),
        pltpu.VMEM((NG, XY - 1, 8 * Z, 128), BF),
        pltpu.VMEM((Z, 8 * NG, 128), F32),
        pltpu.VMEM((Z - 1, 8 * NG, 128), F32),
        pltpu.VMEM((FQ, Z - 1, K, PATCH), BF),
        pltpu.VMEM((FQ, Z, K, PATCH), BF),
        pltpu.VMEM((FQ, Z, K, PATCH), BF),
        sem((6,)),
        sem((NG,)),
        sem((NG,)),
        sem((NG,)),
        sem((NG,)),
        sem,
        sem,
        sem,
        sem((len(BG_PARTS),)),
        sem,
        sem,
        sem,
    ]
    analysed = pl.pallas_call(
        kernel,
        name="analysis",
        out_shape=jax.ShapeDtypeStruct((FQ, Z, K, PATCH), BF),
        in_specs=[pl.BlockSpec(memory_space=pl.ANY)] * 6,
        out_specs=pl.BlockSpec(memory_space=pl.ANY),
        scratch_shapes=scratch,
        compiler_params=pltpu.CompilerParams(collective_id=0, has_side_effects=True, vmem_limit_bytes=VMEM_LIMIT),
    )(
        background,
        perturbation,
        route_dest.T,
        obs_weight.reshape(1, OBS),
        innovation.reshape(1, OBS),
        localization,
    )
    return pl.pallas_call(
        unpack,
        name="unpack",
        out_shape=jax.ShapeDtypeStruct(background.shape, BF),
        in_specs=[pl.BlockSpec(memory_space=pl.ANY)],
        out_specs=pl.BlockSpec(memory_space=pl.ANY),
        scratch_shapes=[
            pltpu.VMEM((FQ, Z, K, PATCH), BF),
            pltpu.VMEM((FL, FL, Z * PATCH), BF),
            sem((Z,)),
            sem((Z,)),
        ],
        compiler_params=pltpu.CompilerParams(vmem_limit_bytes=VMEM_LIMIT),
    )(analysed)


def solution(mesh):
    in_specs = (
        P("member", None, "space"),
        P(None, ("member", "space")),
        P(("member", "space")),
        P(("member", "space")),
        P(("member", "space"), None),
        P(None, None, ("member", "space")),
    )
    out_specs = P("member", None, "space")
    return jax.shard_map(per_device, mesh=mesh, in_specs=in_specs, out_specs=out_specs, check_vma=False)
```

```python
import math

import jax
import jax.numpy as jnp
from jax import lax
from jax.experimental import pallas as pl
from jax.experimental.pallas import tpu as pltpu
from jax.sharding import PartitionSpec as P

BF = jnp.bfloat16
F32 = jnp.float32
MESH = pl.DeviceIdType.MESH
NN = (((1,), (0,)), ((), ()))
NT = (((1,), (1,)), ((), ()))

K = 80
OBS = 4096
UNITS = 128
Z = 4
XY = 16
HALF = UNITS // 2
FL = 20
FQ = 5
PATCH = 512
NS_STEPS = 8
BG_PARTS = ((0, 4), (4, FQ))
BACK_PARTS = ((0, 1), (1, 3), (3, FQ))
VMEM_LIMIT = 63 << 20

GROUPS = (
    ((0, 0, 80), (32, 32, 48)),
    ((8, 8, 72), (24, 24, 56)),
    ((16, 16, 64), (40, 40, 40), (56, 56, 24)),
    ((48, 48, 32), (64, 64, 16), (72, 72, 8)),
)
NG = len(GROUPS)
WIDTH = tuple(sum(n for _, _, n in blocks) for blocks in GROUPS)
RHS_LANE = WIDTH[-1]


def iota(shape, dim):
    return lax.broadcasted_iota(jnp.int32, shape, dim)


def dot(a, b, dims=NN, precision=None):
    return lax.dot_general(a, b, dims, preferred_element_type=F32, precision=precision)


def dot_split(a, b):
    a_high, b_high = a.astype(BF), b.astype(BF)
    a_low, b_low = (a - a_high.astype(F32)).astype(BF), (b - b_high.astype(F32)).astype(BF)
    stacked = dot(jnp.concatenate([a_high, a_low], axis=0), b_high)
    rows = a.shape[0]
    return stacked[:rows] + (dot(a_high, b_low) + stacked[rows:])


def build_weights(dest, weight, localization, innovation, target):
    step = 512
    row = iota((UNITS, 1), 0)
    unit = (row % Z) * 32 + ((row % HALF) // Z) * 2 + row // HALF
    for start in range(0, OBS, step):
        at = slice(start, start + step)
        first = weight[:, at] * localization[0, :, at]
        second = weight[:, at] * localization[1, :, at]
        if innovation is not None:
            first, second = first * innovation[:, at], second * innovation[:, at]
        first, second = first.astype(BF).astype(F32), second.astype(BF).astype(F32)
        chosen = jnp.where(dest[0:1, at] == unit, first, jnp.where(dest[1:2, at] == unit, second, 0.0))
        target[:, at] = chosen.astype(BF)


def build_products(y, feats, group):
    step = 512
    for start in range(0, OBS, step):
        at = slice(start, start + step)
        row = 0
        for i in range(8):
            for k, l, n in GROUPS[group]:
                feats[row : row + n, at] = y[k + i : k + i + 1, at] * y[l : l + n, at]
                row += n


def inverse_root(system):
    eye = (iota((K, K), 0) == iota((K, K), 1)).astype(F32)
    upper = jnp.max(jnp.sum(jnp.abs(system), axis=1, keepdims=True), axis=0, keepdims=True)
    low = jnp.sqrt((K - 1.0) / upper)
    approx, inverse = system * (1.0 / upper), None
    for step in range(NS_STEPS):
        square = 3.0 / (1.0 + low + low * low)
        stretch = jnp.sqrt(square)
        product = approx if inverse is None else dot_split(inverse, approx)
        half = (1.5 * stretch) * eye - (0.5 * stretch * square) * product
        low = 0.5 * stretch * low * (3.0 - square * low * low)
        if step < NS_STEPS - 1:
            approx = dot_split(approx, half)
        inverse = half if inverse is None else dot_split(half, inverse)
    return inverse * lax.rsqrt(upper)


def unpack_system(total):
    lane = iota((8, 128), 1)
    tiles = [None] * (K // 8)
    for g, blocks in enumerate(GROUPS):
        slots = total[8 * g : 8 * g + 8]
        offset = 0
        for k, l, n in blocks:
            rolled = pltpu.roll(slots, (l - offset) % 128, 1) if l != offset else slots
            tiles[k // 8] = jnp.where((lane >= l) & (lane < l + n), rolled, 0.0)
            offset += n
    upper = jnp.concatenate(tiles + [jnp.zeros((128 - K, 128), F32)], axis=0)
    row, col = iota((128, 128), 0), iota((128, 128), 1)
    above = jnp.where((row // 8) == (col // 8), 0.0, upper)
    gram = (upper + above.T)[:K, :K]
    eye = (iota((K, K), 0) == iota((K, K), 1)).astype(F32)
    slots = total[8 * (NG - 1) :]
    part = jnp.zeros((8, 128), F32)
    for i in range(K // 16):
        rolled = pltpu.roll(slots, (16 * i - RHS_LANE) % 128, 1) + pltpu.roll(slots, (16 * i - RHS_LANE - 16) % 128, 1)
        part = jnp.where((iota((8, 128), 0) == i) & (lane // 16 == i), rolled, part)
    right_side = jnp.sum(part, axis=0, keepdims=True)[:, :K]
    return gram + (K - 1.0) * eye, right_side


def mixing_t(root, right_side):
    halfway = jnp.sum(root * right_side, axis=1, keepdims=True)
    mean = jnp.sum(root * halfway, axis=0, keepdims=True)
    spread = math.sqrt(K - 1.0) * root
    row_sum = jnp.sum(root, axis=1, keepdims=True)
    column = jnp.sum(row_sum * halfway, axis=0, keepdims=True) + math.sqrt(K - 1.0) * row_sum
    return (mean + spread + (1.0 - column) / K).astype(BF)


def kernel(
    bg, y_in, dest_in, weight_in, innovation_in, local_in, out,
    bgv, y, dest, weight, innovation, local, coef, weighted, feats,
    stage, peer_stage, stage16, plane, zsend, zrecv, prep, land, back,
    in_sem, core_s, core_r, plane_s, plane_r, z_s, z_r, bg_s, bg_r, back_s, back_r, own_s,
):
    z = lax.axis_index("member")
    s = lax.axis_index("space")
    core = lax.rem(s, 2)
    xy = lax.div(s, 2)

    def z_peer(d):
        return (lax.rem(z + d, Z), s)

    def plane_chip(d):
        return lax.rem(lax.div(xy, 4) + d // 4, 4) * 4 + lax.rem(lax.rem(xy, 4) + d % 4, 4)

    def plane_peer(d):
        return (z, 2 * plane_chip(d) + core)

    core_peer = (z, 2 * xy + 1 - core)

    loads = [
        pltpu.make_async_copy(src, dst, in_sem.at[i])
        for i, (src, dst) in enumerate(
            ((dest_in, dest), (weight_in, weight), (local_in, local), (innovation_in, innovation), (y_in, y), (bg, bgv))
        )
    ]
    for load in loads:
        load.start()

    barrier = pltpu.get_barrier_semaphore()
    far_first = sorted(range(1, XY), key=lambda d: -(min(d // 4, 4 - d // 4) + min(d % 4, 4 - d % 4)))
    peers = [plane_peer(d) for d in far_first] + [z_peer(d) for d in (2, 1, 3)] + [core_peer]
    for peer in peers:
        pl.semaphore_signal(barrier, inc=1, device_id=peer, device_id_type=MESH)


    def remote(src, dst, send, recv, peer):
        return pltpu.make_async_remote_copy(src, dst, send, recv, device_id=peer, device_id_type=MESH)

    branch = pl.when(z >= 0)

    def send_bg(part):
        fqs = slice(*BG_PARTS[part])

        @branch
        def _():
            for d in (2, 1, 3):
                remote(prep.at[fqs, d - 1], land.at[fqs, z], bg_s, bg_r.at[part], z_peer(d)).start()

    def bg_arrivals(part):
        fqs = slice(*BG_PARTS[part])
        return remote(prep.at[fqs], land.at[fqs, 0 : Z - 1], bg_s, bg_r.at[part], z_peer(1))

    def bg_sends():
        return remote(prep, prep, bg_s, bg_r.at[0], z_peer(1))

    def core_copy(g):
        return remote(stage.at[g, 1 - core], peer_stage.at[g], core_s.at[g], core_r.at[g], core_peer)

    def send_core(g):
        @branch
        def _():
            core_copy(g).start()

    def send_plane(g):
        core_copy(g).wait_recv()
        total = stage[g, core] + peer_stage[g]
        if g == NG - 1:
            rest = pltpu.roll(total - total.astype(BF).astype(F32), 16, 1)
            lane = iota(total.shape, 1)
            total = jnp.where((lane >= RHS_LANE + 16) & (lane < RHS_LANE + 32), rest, total)
        stage16[g] = total.reshape(XY, 8 * Z, 128).astype(BF)

        @branch
        def _():
            for d in far_first:
                remote(stage16.at[g, plane_chip(d)], plane.at[g, d - 1], plane_s.at[g], plane_r.at[g], plane_peer(d)).start()

    def plane_all(g):
        return remote(plane.at[g], plane.at[g], plane_s.at[g], plane_r.at[g], plane_peer(1))

    def send_column():
        @branch
        def _():
            for d in (2, 1, 3):
                remote(zsend.at[lax.rem(z + d, Z)], zrecv.at[d - 1], z_s, z_r, z_peer(d)).start()

    def column_all():
        return remote(zrecv, zrecv, z_s, z_r, z_peer(1))

    def own_copy(fqs):
        return pltpu.make_async_copy(back.at[fqs, z], out.at[fqs, z], own_s)

    def send_back(part):
        fqs = slice(*BACK_PARTS[part])

        @branch
        def _():
            for d in (2, 1, 3):
                remote(back.at[fqs, lax.rem(z + d, Z)], out.at[fqs, z], back_s, back_r, z_peer(d)).start()
            own_copy(fqs).start()

    def back_all():
        return remote(back.at[:, 0 : Z - 1], out.at[:, 0 : Z - 1], back_s, back_r, z_peer(1))

    def own_all():
        return pltpu.make_async_copy(back.at[:, 0], out.at[:, 0], own_s)

    def partial_gram(g):
        width = WIDTH[g]
        buf = feats.at[g % 2]
        build_products(y, buf, g)
        tail = None
        if g == NG - 1:
            tail = dot(y[...], weighted[...], NT)
        for part in range(2):
            rows = 4 * width
            result = dot(buf[part * rows : (part + 1) * rows, :], coef[...], NT)
            for j in range(4):
                i = 4 * part + j
                slot = result[j * width : (j + 1) * width]
                if width < 128:
                    pieces = [slot]
                    filled = width
                    if i < K // 16:
                        pieces.append(tail[16 * i : 16 * i + 16])
                        filled += 16
                    pieces.append(jnp.zeros((128 - filled, UNITS), F32))
                    slot = jnp.concatenate(pieces, axis=0)
                turned = slot.T
                stage[g, 0, pl.ds(i, HALF, stride=8), :] = turned[:HALF]
                stage[g, 1, pl.ds(i, HALF, stride=8), :] = turned[HALF:]

    def sum_plane(g):
        plane_all(g).wait_recv()
        total = stage16[g, xy].astype(F32)
        for d in range(XY - 1):
            total = total + plane[g, d].astype(F32)
        for t in range(Z):
            zsend[t, 8 * g : 8 * g + 8] = total[8 * t : 8 * t + 8]

    for load in loads[:4]:
        load.wait()
    build_weights(dest, weight, local, None, coef)
    build_weights(dest, weight, local, innovation, weighted)
    loads[4].wait()
    partial_gram(0)
    loads[5].wait()
    for fq in range(FQ):
        rows = slice(4 * fq, 4 * fq + 4)
        for j in range(FL):
            to = slice(4 * j, 4 * j + 4)
            land[fq, z, to] = bgv[j, rows, pl.ds(pl.multiple_of(z * PATCH, PATCH), PATCH)]
            for d in range(1, Z):
                cells = pl.ds(pl.multiple_of(lax.rem(z + d, Z) * PATCH, PATCH), PATCH)
                prep[fq, d - 1, to] = bgv[j, rows, cells]

    pl.semaphore_wait(barrier, len(peers))
    send_core(0)
    send_bg(0)
    for g in range(1, NG):
        partial_gram(g)
        send_core(g)
        send_plane(g - 1)
    send_plane(NG - 1)
    expand_t = (iota((K, 4 * K), 0) == (iota((K, 4 * K), 1) // 4)).astype(BF)
    for g in range(NG):
        sum_plane(g)
    send_column()
    send_bg(1)
    total = zsend[z]
    column_all().wait_recv()
    for d in range(Z - 1):
        total = total + zrecv[d]

    system, right_side = unpack_system(total)
    mixing = mixing_t(inverse_root(system), right_side)
    wide = jnp.broadcast_to(dot(mixing, expand_t)[:, None, :], (K, 4, 4 * K)).reshape(4 * K, 4 * K)
    same = (iota((4 * K, 4 * K), 0) % 4) == (iota((4 * K, 4 * K), 1) % 4)
    spread = jnp.where(same, wide, 0.0).astype(BF)

    bg_arrivals(0).wait_recv()
    for part, (first, last) in enumerate(BACK_PARTS):
        if last == FQ:
            bg_arrivals(1).wait_recv()
        for fq in range(first, last):
            block = dot(spread, land[fq].reshape(Z * K, PATCH))
            back[fq] = block.astype(BF).reshape(Z, K, PATCH)
        send_back(part)

    for g in range(NG):
        core_copy(g).wait_send()
        plane_all(g).wait_send()
    column_all().wait_send()
    bg_sends().wait_send()
    own_all().wait()
    back_all().wait()


def unpack(dense, out, piece, whole, load_sem, store_sem):
    loads = [pltpu.make_async_copy(dense.at[:, m], piece.at[:, m], load_sem.at[m]) for m in range(Z)]
    for load in loads:
        load.start()
    stores = []
    for m in range(Z):
        loads[m].wait()
        cells = slice(m * PATCH, (m + 1) * PATCH)
        for fq in range(FQ):
            for j in range(FL):
                whole[j, 4 * fq : 4 * fq + 4, cells] = piece[fq, m, 4 * j : 4 * j + 4]
        stores.append(pltpu.make_async_copy(whole.at[:, :, cells], out.at[:, :, cells], store_sem.at[m]))
        stores[-1].start()
    for store in stores:
        store.wait()


def per_device(background, perturbation, innovation, obs_weight, route_dest, localization):
    sem = pltpu.SemaphoreType.DMA
    scratch = [
        pltpu.VMEM((FL, FL, Z * PATCH), BF),
        pltpu.VMEM((K, OBS), BF),
        pltpu.VMEM((2, OBS), jnp.int32),
        pltpu.VMEM((1, OBS), F32),
        pltpu.VMEM((1, OBS), F32),
        pltpu.VMEM((2, 1, OBS), F32),
        pltpu.VMEM((UNITS, OBS), BF),
        pltpu.VMEM((UNITS, OBS), BF),
        pltpu.VMEM((2, 8 * 128, OBS), BF),
        pltpu.VMEM((NG, 2, HALF * 8, 128), F32),
        pltpu.VMEM((NG, HALF * 8, 128), F32),
        pltpu.VMEM((NG, XY, 8 * Z, 128), BF),
        pltpu.VMEM((NG, XY - 1, 8 * Z, 128), BF),
        pltpu.VMEM((Z, 8 * NG, 128), F32),
        pltpu.VMEM((Z - 1, 8 * NG, 128), F32),
        pltpu.VMEM((FQ, Z - 1, K, PATCH), BF),
        pltpu.VMEM((FQ, Z, K, PATCH), BF),
        pltpu.VMEM((FQ, Z, K, PATCH), BF),
        sem((6,)),
        sem((NG,)),
        sem((NG,)),
        sem((NG,)),
        sem((NG,)),
        sem,
        sem,
        sem,
        sem((len(BG_PARTS),)),
        sem,
        sem,
        sem,
    ]
    analysed = pl.pallas_call(
        kernel,
        name="analysis",
        out_shape=jax.ShapeDtypeStruct((FQ, Z, K, PATCH), BF),
        in_specs=[pl.BlockSpec(memory_space=pl.ANY)] * 6,
        out_specs=pl.BlockSpec(memory_space=pl.ANY),
        scratch_shapes=scratch,
        compiler_params=pltpu.CompilerParams(collective_id=0, has_side_effects=True, vmem_limit_bytes=VMEM_LIMIT),
    )(
        background,
        perturbation,
        route_dest.T,
        obs_weight.reshape(1, OBS),
        innovation.reshape(1, OBS),
        localization,
    )
    return pl.pallas_call(
        unpack,
        name="unpack",
        out_shape=jax.ShapeDtypeStruct(background.shape, BF),
        in_specs=[pl.BlockSpec(memory_space=pl.ANY)],
        out_specs=pl.BlockSpec(memory_space=pl.ANY),
        scratch_shapes=[
            pltpu.VMEM((FQ, Z, K, PATCH), BF),
            pltpu.VMEM((FL, FL, Z * PATCH), BF),
            sem((Z,)),
            sem((Z,)),
        ],
        compiler_params=pltpu.CompilerParams(vmem_limit_bytes=VMEM_LIMIT),
    )(analysed)


def solution(mesh):
    in_specs = (
        P("member", None, "space"),
        P(None, ("member", "space")),
        P(("member", "space")),
        P(("member", "space")),
        P(("member", "space"), None),
        P(None, None, ("member", "space")),
    )
    out_specs = P("member", None, "space")
    return jax.shard_map(per_device, mesh=mesh, in_specs=in_specs, out_specs=out_specs, check_vma=False)
```

```python
import math

import jax
import jax.numpy as jnp
from jax import lax
from jax.experimental import pallas as pl
from jax.experimental.pallas import tpu as pltpu
from jax.sharding import PartitionSpec as P

BF = jnp.bfloat16
F32 = jnp.float32
MESH = pl.DeviceIdType.MESH
NN = (((1,), (0,)), ((), ()))
NT = (((1,), (1,)), ((), ()))

K = 80
OBS = 4096
UNITS = 128
Z = 4
XY = 16
HALF = UNITS // 2
FL = 20
FQ = 5
PATCH = 512
NS_STEPS = 8
BG_PARTS = ((0, 4), (4, FQ))
BACK_PARTS = ((0, 1), (1, 3), (3, FQ))
VMEM_LIMIT = 63 << 20

GROUPS = (
    ((0, 0, 80), (32, 32, 48)),
    ((8, 8, 72), (24, 24, 56)),
    ((16, 16, 64), (40, 40, 40), (56, 56, 24)),
    ((48, 48, 32), (64, 64, 16), (72, 72, 8)),
)
NG = len(GROUPS)
PLANE_PARTS = ((0, 2), (2, 3), (3, NG))
WIDTH = tuple(sum(n for _, _, n in blocks) for blocks in GROUPS)
RHS_LANE = WIDTH[-1]


def iota(shape, dim):
    return lax.broadcasted_iota(jnp.int32, shape, dim)


def dot(a, b, dims=NN, precision=None):
    return lax.dot_general(a, b, dims, preferred_element_type=F32, precision=precision)


def dot_split(a, b):
    a_high, b_high = a.astype(BF), b.astype(BF)
    a_low, b_low = (a - a_high.astype(F32)).astype(BF), (b - b_high.astype(F32)).astype(BF)
    stacked = dot(jnp.concatenate([a_high, a_low], axis=0), b_high)
    rows = a.shape[0]
    return stacked[:rows] + (dot(a_high, b_low) + stacked[rows:])


def build_weights(dest, weight, localization, innovation, target):
    step = 512
    row = iota((UNITS, 1), 0)
    unit = (row % Z) * 32 + ((row % HALF) // Z) * 2 + row // HALF
    for start in range(0, OBS, step):
        at = slice(start, start + step)
        first = weight[:, at] * localization[0, :, at]
        second = weight[:, at] * localization[1, :, at]
        if innovation is not None:
            first, second = first * innovation[:, at], second * innovation[:, at]
        first, second = first.astype(BF).astype(F32), second.astype(BF).astype(F32)
        chosen = jnp.where(dest[0:1, at] == unit, first, jnp.where(dest[1:2, at] == unit, second, 0.0))
        target[:, at] = chosen.astype(BF)


def build_products(y, feats, group):
    step = 512
    for start in range(0, OBS, step):
        at = slice(start, start + step)
        row = 0
        for i in range(8):
            for k, l, n in GROUPS[group]:
                feats[row : row + n, at] = y[k + i : k + i + 1, at] * y[l : l + n, at]
                row += n


def inverse_root(system):
    eye = (iota((K, K), 0) == iota((K, K), 1)).astype(F32)
    upper = jnp.max(jnp.sum(jnp.abs(system), axis=1, keepdims=True), axis=0, keepdims=True)
    low = jnp.sqrt((K - 1.0) / upper)
    approx, inverse = system * (1.0 / upper), None
    for step in range(NS_STEPS):
        square = 3.0 / (1.0 + low + low * low)
        stretch = jnp.sqrt(square)
        product = approx if inverse is None else dot_split(inverse, approx)
        half = (1.5 * stretch) * eye - (0.5 * stretch * square) * product
        low = 0.5 * stretch * low * (3.0 - square * low * low)
        if step < NS_STEPS - 1:
            approx = dot_split(approx, half)
        inverse = half if inverse is None else dot_split(half, inverse)
    return inverse * lax.rsqrt(upper)


def unpack_system(total):
    lane = iota((8, 128), 1)
    tiles = [None] * (K // 8)
    for g, blocks in enumerate(GROUPS):
        slots = total[8 * g : 8 * g + 8]
        offset = 0
        for k, l, n in blocks:
            rolled = pltpu.roll(slots, (l - offset) % 128, 1) if l != offset else slots
            tiles[k // 8] = jnp.where((lane >= l) & (lane < l + n), rolled, 0.0)
            offset += n
    upper = jnp.concatenate(tiles + [jnp.zeros((128 - K, 128), F32)], axis=0)
    row, col = iota((128, 128), 0), iota((128, 128), 1)
    above = jnp.where((row // 8) == (col // 8), 0.0, upper)
    gram = (upper + above.T)[:K, :K]
    eye = (iota((K, K), 0) == iota((K, K), 1)).astype(F32)
    slots = total[8 * (NG - 1) :]
    part = jnp.zeros((8, 128), F32)
    for i in range(K // 16):
        rolled = pltpu.roll(slots, (16 * i - RHS_LANE) % 128, 1) + pltpu.roll(slots, (16 * i - RHS_LANE - 16) % 128, 1)
        part = jnp.where((iota((8, 128), 0) == i) & (lane // 16 == i), rolled, part)
    right_side = jnp.sum(part, axis=0, keepdims=True)[:, :K]
    return gram + (K - 1.0) * eye, right_side


def mixing_t(root, right_side):
    halfway = jnp.sum(root * right_side, axis=1, keepdims=True)
    mean = jnp.sum(root * halfway, axis=0, keepdims=True)
    spread = math.sqrt(K - 1.0) * root
    row_sum = jnp.sum(root, axis=1, keepdims=True)
    column = jnp.sum(row_sum * halfway, axis=0, keepdims=True) + math.sqrt(K - 1.0) * row_sum
    return (mean + spread + (1.0 - column) / K).astype(BF)


def kernel(
    bg, y_in, dest_in, weight_in, innovation_in, local_in, out,
    bgv, y, dest, weight, innovation, local, coef, weighted, feats,
    stage, peer_stage, stage16, plane, zsend, zrecv, prep, land, back,
    in_sem, core_s, core_r, plane_s, plane_r, z_s, z_r, bg_s, bg_r, back_s, back_r, own_s,
):
    z = lax.axis_index("member")
    s = lax.axis_index("space")
    core = lax.rem(s, 2)
    xy = lax.div(s, 2)

    def z_peer(d):
        return (lax.rem(z + d, Z), s)

    def plane_chip(d):
        return lax.rem(lax.div(xy, 4) + d // 4, 4) * 4 + lax.rem(lax.rem(xy, 4) + d % 4, 4)

    def plane_peer(d):
        return (z, 2 * plane_chip(d) + core)

    core_peer = (z, 2 * xy + 1 - core)

    loads = [
        pltpu.make_async_copy(src, dst, in_sem.at[i])
        for i, (src, dst) in enumerate(
            ((dest_in, dest), (weight_in, weight), (local_in, local), (innovation_in, innovation), (y_in, y), (bg, bgv))
        )
    ]
    for load in loads:
        load.start()

    barrier = pltpu.get_barrier_semaphore()
    far_first = sorted(range(1, XY), key=lambda d: -(min(d // 4, 4 - d // 4) + min(d % 4, 4 - d % 4)))
    peers = [plane_peer(d) for d in far_first] + [z_peer(d) for d in (2, 1, 3)] + [core_peer]
    for peer in peers:
        pl.semaphore_signal(barrier, inc=1, device_id=peer, device_id_type=MESH)


    def remote(src, dst, send, recv, peer):
        return pltpu.make_async_remote_copy(src, dst, send, recv, device_id=peer, device_id_type=MESH)

    branch = pl.when(z >= 0)

    def send_bg(part):
        fqs = slice(*BG_PARTS[part])

        @branch
        def _():
            for d in (2, 1, 3):
                remote(prep.at[fqs, d - 1], land.at[fqs, z], bg_s, bg_r.at[part], z_peer(d)).start()

    def bg_arrivals(part):
        fqs = slice(*BG_PARTS[part])
        return remote(prep.at[fqs], land.at[fqs, 0 : Z - 1], bg_s, bg_r.at[part], z_peer(1))

    def bg_sends():
        return remote(prep, prep, bg_s, bg_r.at[0], z_peer(1))

    def core_copy(g):
        return remote(stage.at[g, 1 - core], peer_stage.at[g], core_s.at[g], core_r.at[g], core_peer)

    def send_core(g):
        @branch
        def _():
            core_copy(g).start()

    def join_cores(g):
        core_copy(g).wait_recv()
        total = stage[g, core] + peer_stage[g]
        if g == NG - 1:
            rest = pltpu.roll(total - total.astype(BF).astype(F32), 16, 1)
            lane = iota(total.shape, 1)
            total = jnp.where((lane >= RHS_LANE + 16) & (lane < RHS_LANE + 32), rest, total)
        stage16[:, g] = total.reshape(XY, 8 * Z, 128).astype(BF)

    def send_plane(part):
        groups = slice(*PLANE_PARTS[part])

        @branch
        def _():
            for d in far_first:
                remote(
                    stage16.at[plane_chip(d), groups], plane.at[d - 1, groups], plane_s.at[part], plane_r.at[part], plane_peer(d)
                ).start()

    def plane_all(part):
        arrived = plane.at[:, slice(*PLANE_PARTS[part])]
        return remote(arrived, arrived, plane_s.at[part], plane_r.at[part], plane_peer(1))

    def send_column():
        @branch
        def _():
            for d in (2, 1, 3):
                remote(zsend.at[lax.rem(z + d, Z)], zrecv.at[d - 1], z_s, z_r, z_peer(d)).start()

    def column_all():
        return remote(zrecv, zrecv, z_s, z_r, z_peer(1))

    def own_copy(fqs):
        return pltpu.make_async_copy(back.at[fqs, z], out.at[fqs, z], own_s)

    def send_back(part):
        fqs = slice(*BACK_PARTS[part])

        @branch
        def _():
            for d in (2, 1, 3):
                remote(back.at[fqs, lax.rem(z + d, Z)], out.at[fqs, z], back_s, back_r, z_peer(d)).start()
            own_copy(fqs).start()

    def back_all():
        return remote(back.at[:, 0 : Z - 1], out.at[:, 0 : Z - 1], back_s, back_r, z_peer(1))

    def own_all():
        return pltpu.make_async_copy(back.at[:, 0], out.at[:, 0], own_s)

    def partial_gram(g):
        width = WIDTH[g]
        buf = feats.at[g % 2]
        build_products(y, buf, g)
        tail = None
        if g == NG - 1:
            tail = dot(y[...], weighted[...], NT)
        for part in range(2):
            rows = 4 * width
            result = dot(buf[part * rows : (part + 1) * rows, :], coef[...], NT)
            for j in range(4):
                i = 4 * part + j
                slot = result[j * width : (j + 1) * width]
                if width < 128:
                    pieces = [slot]
                    filled = width
                    if i < K // 16:
                        pieces.append(tail[16 * i : 16 * i + 16])
                        filled += 16
                    pieces.append(jnp.zeros((128 - filled, UNITS), F32))
                    slot = jnp.concatenate(pieces, axis=0)
                turned = slot.T
                stage[g, 0, pl.ds(i, HALF, stride=8), :] = turned[:HALF]
                stage[g, 1, pl.ds(i, HALF, stride=8), :] = turned[HALF:]

    def sum_plane(g):
        total = stage16[xy, g].astype(F32)
        for d in range(XY - 1):
            total = total + plane[d, g].astype(F32)
        for t in range(Z):
            zsend[t, 8 * g : 8 * g + 8] = total[8 * t : 8 * t + 8]

    for load in loads[:4]:
        load.wait()
    build_weights(dest, weight, local, None, coef)
    build_weights(dest, weight, local, innovation, weighted)
    loads[4].wait()
    partial_gram(0)
    loads[5].wait()
    for fq in range(FQ):
        rows = slice(4 * fq, 4 * fq + 4)
        for j in range(FL):
            to = slice(4 * j, 4 * j + 4)
            land[fq, z, to] = bgv[j, rows, pl.ds(pl.multiple_of(z * PATCH, PATCH), PATCH)]
            for d in range(1, Z):
                cells = pl.ds(pl.multiple_of(lax.rem(z + d, Z) * PATCH, PATCH), PATCH)
                prep[fq, d - 1, to] = bgv[j, rows, cells]

    pl.semaphore_wait(barrier, len(peers))
    send_core(0)
    send_bg(0)
    for g in range(1, NG):
        partial_gram(g)
        send_core(g)
        join_cores(g - 1)
        for part, (_, last) in enumerate(PLANE_PARTS):
            if last == g:
                send_plane(part)
    join_cores(NG - 1)
    send_plane(len(PLANE_PARTS) - 1)
    expand_t = (iota((K, 4 * K), 0) == (iota((K, 4 * K), 1) // 4)).astype(BF)
    for part, (first, last) in enumerate(PLANE_PARTS):
        plane_all(part).wait_recv()
        for g in range(first, last):
            sum_plane(g)
    send_column()
    send_bg(1)
    total = zsend[z]
    column_all().wait_recv()
    for d in range(Z - 1):
        total = total + zrecv[d]

    system, right_side = unpack_system(total)
    mixing = mixing_t(inverse_root(system), right_side)
    wide = jnp.broadcast_to(dot(mixing, expand_t)[:, None, :], (K, 4, 4 * K)).reshape(4 * K, 4 * K)
    same = (iota((4 * K, 4 * K), 0) % 4) == (iota((4 * K, 4 * K), 1) % 4)
    spread = jnp.where(same, wide, 0.0).astype(BF)

    bg_arrivals(0).wait_recv()
    for part, (first, last) in enumerate(BACK_PARTS):
        if last == FQ:
            bg_arrivals(1).wait_recv()
        for fq in range(first, last):
            block = dot(spread, land[fq].reshape(Z * K, PATCH))
            back[fq] = block.astype(BF).reshape(Z, K, PATCH)
        send_back(part)

    for g in range(NG):
        core_copy(g).wait_send()
    for part in range(len(PLANE_PARTS)):
        plane_all(part).wait_send()
    column_all().wait_send()
    bg_sends().wait_send()
    own_all().wait()
    back_all().wait()


def unpack(dense, out, piece, whole, load_sem, store_sem):
    loads = [pltpu.make_async_copy(dense.at[:, m], piece.at[:, m], load_sem.at[m]) for m in range(Z)]
    for load in loads:
        load.start()
    stores = []
    for m in range(Z):
        loads[m].wait()
        cells = slice(m * PATCH, (m + 1) * PATCH)
        for fq in range(FQ):
            for j in range(FL):
                whole[j, 4 * fq : 4 * fq + 4, cells] = piece[fq, m, 4 * j : 4 * j + 4]
        stores.append(pltpu.make_async_copy(whole.at[:, :, cells], out.at[:, :, cells], store_sem.at[m]))
        stores[-1].start()
    for store in stores:
        store.wait()


def per_device(background, perturbation, innovation, obs_weight, route_dest, localization):
    sem = pltpu.SemaphoreType.DMA
    scratch = [
        pltpu.VMEM((FL, FL, Z * PATCH), BF),
        pltpu.VMEM((K, OBS), BF),
        pltpu.VMEM((2, OBS), jnp.int32),
        pltpu.VMEM((1, OBS), F32),
        pltpu.VMEM((1, OBS), F32),
        pltpu.VMEM((2, 1, OBS), F32),
        pltpu.VMEM((UNITS, OBS), BF),
        pltpu.VMEM((UNITS, OBS), BF),
        pltpu.VMEM((2, 8 * 128, OBS), BF),
        pltpu.VMEM((NG, 2, HALF * 8, 128), F32),
        pltpu.VMEM((NG, HALF * 8, 128), F32),
        pltpu.VMEM((XY, NG, 8 * Z, 128), BF),
        pltpu.VMEM((XY - 1, NG, 8 * Z, 128), BF),
        pltpu.VMEM((Z, 8 * NG, 128), F32),
        pltpu.VMEM((Z - 1, 8 * NG, 128), F32),
        pltpu.VMEM((FQ, Z - 1, K, PATCH), BF),
        pltpu.VMEM((FQ, Z, K, PATCH), BF),
        pltpu.VMEM((FQ, Z, K, PATCH), BF),
        sem((6,)),
        sem((NG,)),
        sem((NG,)),
        sem((len(PLANE_PARTS),)),
        sem((len(PLANE_PARTS),)),
        sem,
        sem,
        sem,
        sem((len(BG_PARTS),)),
        sem,
        sem,
        sem,
    ]
    analysed = pl.pallas_call(
        kernel,
        name="analysis",
        out_shape=jax.ShapeDtypeStruct((FQ, Z, K, PATCH), BF),
        in_specs=[pl.BlockSpec(memory_space=pl.ANY)] * 6,
        out_specs=pl.BlockSpec(memory_space=pl.ANY),
        scratch_shapes=scratch,
        compiler_params=pltpu.CompilerParams(collective_id=0, has_side_effects=True, vmem_limit_bytes=VMEM_LIMIT),
    )(
        background,
        perturbation,
        route_dest.T,
        obs_weight.reshape(1, OBS),
        innovation.reshape(1, OBS),
        localization,
    )
    return pl.pallas_call(
        unpack,
        name="unpack",
        out_shape=jax.ShapeDtypeStruct(background.shape, BF),
        in_specs=[pl.BlockSpec(memory_space=pl.ANY)],
        out_specs=pl.BlockSpec(memory_space=pl.ANY),
        scratch_shapes=[
            pltpu.VMEM((FQ, Z, K, PATCH), BF),
            pltpu.VMEM((FL, FL, Z * PATCH), BF),
            sem((Z,)),
            sem((Z,)),
        ],
        compiler_params=pltpu.CompilerParams(vmem_limit_bytes=VMEM_LIMIT),
    )(analysed)


def solution(mesh):
    in_specs = (
        P("member", None, "space"),
        P(None, ("member", "space")),
        P(("member", "space")),
        P(("member", "space")),
        P(("member", "space"), None),
        P(None, None, ("member", "space")),
    )
    out_specs = P("member", None, "space")
    return jax.shard_map(per_device, mesh=mesh, in_specs=in_specs, out_specs=out_specs, check_vma=False)
```
